768 devices in a mesh: space: 96 (over z, y), members: 8 (over x, core).
Axes of the slice: x: 4, y: 8, z: 12, core: 2. Of those that a mesh axis runs over, the one named last changes fastest.
Arguments:
- alpha: bfloat16 [2, 80, 768, 128], P(None, 'members', 'space'), may hold values from -6 to 6
- kernel: bfloat16 [1152, 128, 128], P('space'), may hold values from -0.5 to 0.5
- src_index: int32 [1152], P('space'), may hold values from 4 to 19, as said below
- dst_index: int32 [1152], P('space'), may hold values from 0 to 7
- entry_count: int32 [96], P('space'), may hold values from 6 to 12, as said below
- interp_index: int32 [4, 1769472], P(None, 'space'), may hold values from 0 to 1023
- interp_weight: float32 [4, 1769472], P(None, 'space'), may hold values from 0.1 to 1
- perturbation: bfloat16 [2, 80, 1769472], P(None, 'members', 'space'), may hold values from -0.625 to 0.625
Outputs:
- increment: float32 [2, 1769472], P(None, ('space', 'members'))
The draws below stay inside these ranges and needn't reach their ends.
Inputs may be any that keep to these rules, and one draw needn't show every extreme that they name: `src_index`: live entries read either the last 4 blocks of the previous tile, any block of the own tile, or the first 4 blocks of the next tile; padded entries read the own tile's first block. `entry_count`: some tile has all 12 entries live.
All inputs are finite; a program needn't handle non-finite values.
Results may differ from the reference program's by a relative error of at most 0.0029.
Values may be sent and summed in bfloat16 or wider, within the bound.
A program may use at most 128 MiB of HBM per device.

```python
import jax
import jax.numpy as jnp
from jax import lax

BS = 128
NB = 8
HB = 4
LEV = 2
GP = 18432
P_SIZE = 12
MEMBERS = 80
BLOCKS = 768
ENTRIES = 1152
POINTS = 1769472
N_SPACE = 96


def pattern(key):
    keys = jax.random.split(key, 6)
    counts = jax.random.randint(keys[0], (N_SPACE,), P_SIZE // 2, P_SIZE + 1)
    fullest = jax.random.randint(keys[1], (), 0, N_SPACE)
    counts = jnp.where(jnp.arange(N_SPACE) == fullest, P_SIZE, counts)
    side = jax.random.randint(keys[2], (N_SPACE, P_SIZE), 0, 3)
    ends = jax.random.randint(keys[3], (N_SPACE, P_SIZE), 0, HB)
    inner = jax.random.randint(keys[4], (N_SPACE, P_SIZE), 0, NB)
    targets = jax.random.randint(keys[5], (N_SPACE, P_SIZE), 0, NB)
    sources = jnp.where(side == 0, NB - 1 - ends, jnp.where(side == 1, NB + inner, 2 * NB + ends))
    live = jnp.arange(P_SIZE)[None, :] < counts[:, None]
    sources = jnp.where(live, sources, NB)
    targets = jnp.where(live, targets, 0)
    return (sources.reshape(-1).astype(jnp.int32), targets.reshape(-1).astype(jnp.int32), counts.astype(jnp.int32))


def draw_src_index(key, part):
    return pattern(key)[0]


def draw_dst_index(key, part):
    return pattern(key)[1]


def draw_entry_count(key, part):
    return pattern(key)[2]


def place_ends(entries, rng, smallest, high):
    place = [jax.random.randint(jax.random.fold_in(rng, axis), (), 0, length) for axis, length in enumerate(entries.shape)]
    longest = entries.shape.index(max(entries.shape))
    neighbour = place[:longest] + [(place[longest] + 1) % entries.shape[longest]] + place[longest + 1:]
    return entries.at[tuple(place)].set(smallest).at[tuple(neighbour)].set(high)


def block_scale(rng, shape, cuts, low, largest):
    def one(dim, shards_of):
        steps = jax.random.uniform(jax.random.fold_in(jax.random.fold_in(rng, 6), dim), (shards_of,), jnp.float32, low / len(cuts), largest / len(cuts))
        return jnp.repeat(jnp.exp(steps), shape[dim] // shards_of).reshape((-1,) + (1,) * (len(shape) - dim - 1))

    gain = one(*cuts[0])
    for cut in cuts[1:]:
        gain = gain * one(*cut)
    return gain


def gaussian(stream_key, shape, width, bound, shards=(), held_as=jnp.bfloat16):
    factor_of = block_scale(stream_key, shape, shards, -0.22, 0.18) if shards else 1.0
    values = jax.random.normal(stream_key, shape, jnp.float32) * width * factor_of
    return jnp.minimum(jnp.maximum(values, -bound), bound).astype(held_as)


def setup_inputs(seed: int = 0) -> dict:
    splits = jax.random.split(jax.random.key(seed), 9)
    return {
        "alpha": gaussian(splits[0], (LEV, MEMBERS, BLOCKS, BS), 1.0, 6.0, ((1, 8), (2, 96))),
        "kernel": gaussian(splits[1], (ENTRIES, BS, BS), BS ** -0.5, 0.5, ((0, 96),)),
        "src_index": draw_src_index(jax.random.fold_in(splits[8], 71), 0),
        "dst_index": draw_dst_index(jax.random.fold_in(splits[8], 71), 0),
        "entry_count": draw_entry_count(jax.random.fold_in(splits[8], 71), 0),
        "interp_index": place_ends(jax.random.randint(splits[5], (4, POINTS), 0, NB * BS), jax.random.fold_in(splits[5], 1), 0, (NB * BS) - 1).astype(jnp.int32),
        "interp_weight": jnp.clip(0.1 + 0.9 * jax.random.uniform(splits[6], (4, POINTS), jnp.float32) ** block_scale(splits[6], (4, POINTS), ((1, 96),), -0.2, 0.2), 0.1, 1.0),
        "perturbation": gaussian(splits[7], (LEV, MEMBERS, POINTS), MEMBERS ** -0.5, 0.625, ((1, 8), (2, 96))),
    }


def reference(alpha, kernel, src_index, dst_index, entry_count, interp_index, interp_weight, perturbation):
    def one_tile(tile):
        kernels = lax.dynamic_slice_in_dim(kernel, tile * P_SIZE, P_SIZE, 0).astype(jnp.float32)
        sources = lax.dynamic_slice_in_dim(src_index, tile * P_SIZE, P_SIZE, 0)
        targets = lax.dynamic_slice_in_dim(dst_index, tile * P_SIZE, P_SIZE, 0)
        count = lax.dynamic_slice_in_dim(entry_count, tile, 1, 0)[0]
        side = sources // NB
        within = sources % NB
        global_block = (((tile + side - 1) % N_SPACE) * NB + within).astype(jnp.int32)
        pieces = jnp.take(alpha, global_block, axis=2).astype(jnp.float32)
        product = jnp.einsum("lmpq,pqr->lmpr", pieces, kernels, precision=lax.Precision.HIGHEST)
        live = (jnp.arange(P_SIZE, dtype=jnp.int32) < count).astype(jnp.float32)
        onehot = (targets[:, None] == jnp.arange(NB, dtype=jnp.int32)[None, :]).astype(jnp.float32) * live[:, None]
        summed = jnp.einsum("lmpr,pj->lmjr", product, onehot, precision=lax.Precision.HIGHEST)
        convolved = summed.astype(jnp.bfloat16).reshape(LEV, MEMBERS, NB * BS)
        stencil = lax.dynamic_slice_in_dim(interp_index, tile * GP, GP, 1)
        weights = lax.dynamic_slice_in_dim(interp_weight, tile * GP, GP, 1)
        values = jnp.take(convolved, stencil, axis=2)
        interpolated = jnp.sum(values.astype(jnp.float32) * weights[None, None], axis=2)
        members_here = lax.dynamic_slice_in_dim(perturbation, tile * GP, GP, 2)
        return jnp.sum(members_here.astype(jnp.float32) * interpolated, axis=1)

    tiles = lax.map(one_tile, jnp.arange(N_SPACE, dtype=jnp.int32))
    return jnp.transpose(tiles, (1, 0, 2)).reshape(LEV, N_SPACE * GP)
```

```python
import jax
import jax.numpy as jnp
from jax import lax
from jax.experimental import pallas as pl
from jax.experimental.pallas import tpu as pltpu
from jax.sharding import PartitionSpec as P

MESH = pl.DeviceIdType.MESH
LANES = 128


def halo_kernel(alpha_ref, prev_ref, next_ref, send_sem, recv_sem):
    count = lax.axis_size("space")
    me = lax.axis_index("space")
    right, left = lax.rem(me + 1, count), lax.rem(me + count - 1, count)
    barrier = pltpu.get_barrier_semaphore()
    for neighbour in (left, right):
        pl.semaphore_signal(barrier, inc=1, device_id={"space": neighbour}, device_id_type=MESH)
    pl.semaphore_wait(barrier, 2)
    copies = []
    for way, (neighbour, landing) in enumerate(((right, prev_ref), (left, next_ref))):
        copy = pltpu.make_async_remote_copy(
            src_ref=alpha_ref,
            dst_ref=landing,
            send_sem=send_sem.at[way],
            recv_sem=recv_sem.at[way],
            device_id={"space": neighbour},
            device_id_type=MESH,
        )
        copy.start()
        copies.append(copy)
    for copy in copies:
        copy.wait()


def exchange_halo(alpha):
    vmem = pl.BlockSpec(memory_space=pltpu.VMEM)
    shape = jax.ShapeDtypeStruct(alpha.shape, alpha.dtype)
    return pl.pallas_call(
        halo_kernel,
        out_shape=(shape, shape),
        in_specs=[vmem],
        out_specs=(vmem, vmem),
        scratch_shapes=[pltpu.SemaphoreType.DMA((2,)), pltpu.SemaphoreType.DMA((2,))],
        compiler_params=pltpu.CompilerParams(
            collective_id=0, has_side_effects=True, vmem_limit_bytes=8 * 1024 * 1024
        ),
    )(alpha)


def convolve(src_ref, dst_ref, count_ref, sides, kernel_ref, window, sums, table):
    levels, members, blocks, _ = sides[0].shape
    lm = levels * members
    rows = lm * blocks
    for side, ref in enumerate(sides):
        for l in range(levels):
            for m in range(members):
                at = side * rows + (m * levels + l) * blocks
                window[at:at + blocks, :] = ref[l, m].astype(jnp.float32)
    sums[...] = jnp.zeros_like(sums)
    for e in range(kernel_ref.shape[0]):
        s = src_ref[e]
        start = (s // blocks) * rows + s % blocks
        piece = window[pl.ds(start, lm, stride=blocks), :].astype(jnp.bfloat16)
        product = jnp.dot(piece, kernel_ref[e], preferred_element_type=jnp.float32)
        live = jnp.where(e < count_ref[0], 1.0, 0.0).astype(jnp.float32)
        d = dst_ref[e]
        sums[d] = sums[d] + product * live
    half = blocks // 2
    for j in range(blocks):
        table[j // half, pl.ds(j % half, lm, stride=half), :] = sums[j]


def interpolate(table, index_ref, weight_ref, pert_ref, out_ref):
    members, levels, _ = pert_ref.shape
    owners, _, span = out_ref.shape
    half = table.shape[1] // (members * levels)
    depth = 2 * LANES
    left = jnp.concatenate([table[0], table[1]], axis=1).astype(jnp.bfloat16)

    def body(g, carry):
        cols = pl.ds(pl.multiple_of(g * span, LANES), span)
        sub = lax.broadcasted_iota(jnp.int32, (levels * half, span), 0) % half
        points = lax.broadcasted_iota(jnp.int16, (depth, span), 0)
        total = None
        for k in range(index_ref.shape[0]):
            index = index_ref[pl.ds(k, 1), cols]
            weight = jnp.broadcast_to(weight_ref[pl.ds(k, 1), cols], (levels * half, span))
            block = index >> 7
            place = (block // half) * LANES + (index & (LANES - 1))
            row = jnp.broadcast_to(block % half, (levels * half, span))
            masked = jnp.where(row == sub, weight, 0.0)
            place = jnp.broadcast_to(place, (16, span)).astype(jnp.int16)[0:1]
            hot = jnp.where(
                points == jnp.broadcast_to(place, (depth, span)), jnp.bfloat16(1), jnp.bfloat16(0)
            )
            values = jnp.dot(left, hot, preferred_element_type=jnp.float32)
            values = values.reshape(members, levels * half, span) * masked[None]
            total = values if k == 0 else total + values
        summed = None
        for m in range(members):
            p = pert_ref[m, :, cols].astype(jnp.float32)
            wide = jnp.concatenate(
                [jnp.broadcast_to(p[l:l + 1], (half, span)) for l in range(levels)], axis=0
            )
            summed = total[m] * wide if m == 0 else summed + total[m] * wide
        out_ref[g] = jnp.concatenate(
            [jnp.sum(summed[l * half:(l + 1) * half], axis=0, keepdims=True) for l in range(levels)], axis=0
        )
        return carry

    lax.fori_loop(0, owners, body, 0)


def local_kernel(
    src_ref, dst_ref, count_ref, prev_ref, alpha_ref, next_ref, kernel_ref, index_ref, weight_ref, pert_ref,
    out_ref, window, sums, table, kernel_vmem, index_vmem, weight_vmem, pert_vmem, load_sem,
):
    loads = []
    pairs = ((kernel_ref, kernel_vmem), (index_ref, index_vmem), (weight_ref, weight_vmem), (pert_ref, pert_vmem))
    for number, (source, target) in enumerate(pairs):
        load = pltpu.make_async_copy(source, target, load_sem.at[number])
        load.start()
        loads.append(load)
    loads[0].wait()
    convolve(src_ref, dst_ref, count_ref, (prev_ref, alpha_ref, next_ref), kernel_vmem, window, sums, table)
    for load in loads[1:]:
        load.wait()
    interpolate(table, index_vmem, weight_vmem, pert_vmem, out_ref)


def local_increment(owners, prev, alpha, following, kernel, src, dst, count, index, weight, pert):
    levels, members, blocks, width = alpha.shape
    lm = levels * members
    smem = pl.BlockSpec(memory_space=pltpu.SMEM)
    vmem = pl.BlockSpec(memory_space=pltpu.VMEM)
    return pl.pallas_call(
        local_kernel,
        out_shape=jax.ShapeDtypeStruct((owners, levels, index.shape[1] // owners), jnp.float32),
        in_specs=[smem] * 3 + [vmem] * 3 + [pl.BlockSpec(memory_space=pl.ANY)] * 4,
        out_specs=vmem,
        scratch_shapes=[
            pltpu.VMEM((3 * lm * blocks, width), jnp.float32),
            pltpu.VMEM((blocks, lm, width), jnp.float32),
            pltpu.VMEM((2, lm * blocks // 2, width), jnp.float32),
            pltpu.VMEM(kernel.shape, kernel.dtype),
            pltpu.VMEM(index.shape, index.dtype),
            pltpu.VMEM(weight.shape, weight.dtype),
            pltpu.VMEM((members, levels, index.shape[1]), pert.dtype),
            pltpu.SemaphoreType.DMA((4,)),
        ],
        compiler_params=pltpu.CompilerParams(vmem_limit_bytes=60 * 1024 * 1024),
    )(src, dst, count, prev, alpha, following, kernel, index, weight, jnp.transpose(pert, (1, 0, 2)))


def share_kernel(owners, partial_ref, out_ref, slots, send_sem, recv_sem):
    me = lax.axis_index("members")
    barrier = pltpu.get_barrier_semaphore()
    for step in range(1, owners):
        peer = lax.rem(me + step, owners)
        pl.semaphore_signal(barrier, inc=1, device_id={"members": peer}, device_id_type=MESH)
    pl.semaphore_wait(barrier, owners - 1)
    copies = []
    for step in range(1, owners):
        peer = lax.rem(me + step, owners)
        copy = pltpu.make_async_remote_copy(
            src_ref=partial_ref.at[peer],
            dst_ref=slots.at[step - 1],
            send_sem=send_sem.at[step - 1],
            recv_sem=recv_sem.at[step - 1],
            device_id={"members": peer},
            device_id_type=MESH,
        )
        copy.start()
        copies.append(copy)
    total = partial_ref[me]
    for step, copy in enumerate(copies):
        copy.wait_recv()
        total = total + slots[step]
    out_ref[...] = total
    for copy in copies:
        copy.wait_send()


def share_increment(partial):
    owners, levels, span = partial.shape
    vmem = pl.BlockSpec(memory_space=pltpu.VMEM)
    return pl.pallas_call(
        lambda *refs: share_kernel(owners, *refs),
        out_shape=jax.ShapeDtypeStruct((levels, span), jnp.float32),
        in_specs=[vmem],
        out_specs=vmem,
        scratch_shapes=[
            pltpu.VMEM((owners - 1, levels, span), jnp.float32),
            pltpu.SemaphoreType.DMA((owners - 1,)),
            pltpu.SemaphoreType.DMA((owners - 1,)),
        ],
        compiler_params=pltpu.CompilerParams(
            collective_id=1, has_side_effects=True, vmem_limit_bytes=8 * 1024 * 1024
        ),
    )(partial)


def per_device(
    alpha, kernel, src_index, dst_index, entry_count, interp_index, interp_weight, perturbation
):
    owners = lax.axis_size("members")
    prev, following = exchange_halo(alpha)
    partial = local_increment(
        owners, prev, alpha, following, kernel, src_index, dst_index, entry_count,
        interp_index, interp_weight, perturbation,
    )
    return share_increment(partial)


def solution(mesh):
    return jax.shard_map(
        per_device,
        mesh=mesh,
        in_specs=(
            P(None, "members", "space", None),
            P("space", None, None),
            P("space"),
            P("space"),
            P("space"),
            P(None, "space"),
            P(None, "space"),
            P(None, "members", "space"),
        ),
        out_specs=P(None, ("space", "members")),
        check_vma=False,
    )
```

```python
import jax
import jax.numpy as jnp
from jax import lax
from jax.experimental import pallas as pl
from jax.experimental.pallas import tpu as pltpu
from jax.sharding import PartitionSpec as P

MESH = pl.DeviceIdType.MESH
LANES = 128


def stage(ref, side, rows, window):
    levels, members, blocks, _ = ref.shape
    for l in range(levels):
        for m in range(members):
            at = (m * levels + l) * blocks
            rows[side, at:at + blocks, :] = ref[l, m].astype(jnp.float32)
    for j in range(blocks):
        window[side * blocks + j] = rows[side, pl.ds(j, levels * members, stride=blocks), :]


def convolve(src_ref, dst_ref, count_ref, blocks, kernel_ref, window, table):
    lm = window.shape[1]
    sums = [jnp.zeros((lm, LANES), jnp.float32) for _ in range(blocks)]
    for e in range(kernel_ref.shape[0]):
        piece = window[src_ref[e]].astype(jnp.bfloat16)
        product = jnp.dot(piece, kernel_ref[e], preferred_element_type=jnp.float32)
        live = jnp.where(e < count_ref[0], 1.0, 0.0).astype(jnp.float32)
        for j in range(blocks):
            factor = jnp.where(dst_ref[e] == j, live, 0.0)
            sums[j] = sums[j] + product * factor
    half = blocks // 2
    for j in range(blocks):
        table[j // half, pl.ds(j % half, lm, stride=half), :] = sums[j]


def interpolate(left, cols, index_ref, weight_ref, pert_ref):
    members, levels, _ = pert_ref.shape
    span = cols.size
    half = left.shape[0] // (members * levels)
    depth = 2 * LANES
    sub = lax.broadcasted_iota(jnp.int32, (levels * half, span), 0) % half
    points = lax.broadcasted_iota(jnp.int16, (depth, span), 0)
    total = None
    for k in range(index_ref.shape[0]):
        index = index_ref[pl.ds(k, 1), cols]
        weight = jnp.broadcast_to(weight_ref[pl.ds(k, 1), cols], (levels * half, span))
        block = index >> 7
        place = (block // half) * LANES + (index & (LANES - 1))
        row = jnp.broadcast_to(block % half, (levels * half, span))
        masked = jnp.where(row == sub, weight, 0.0)
        place = jnp.broadcast_to(place, (16, span)).astype(jnp.int16)[0:1]
        hot = jnp.where(
            points == jnp.broadcast_to(place, (depth, span)), jnp.bfloat16(1), jnp.bfloat16(0)
        )
        values = jnp.dot(left, hot, preferred_element_type=jnp.float32)
        values = values.reshape(members, levels * half, span) * masked[None]
        total = values if k == 0 else total + values
    summed = None
    for m in range(members):
        p = pert_ref[m, :, cols].astype(jnp.float32)
        wide = jnp.concatenate(
            [jnp.broadcast_to(p[l:l + 1], (half, span)) for l in range(levels)], axis=0
        )
        summed = total[m] * wide if m == 0 else summed + total[m] * wide
    return jnp.concatenate(
        [jnp.sum(summed[l * half:(l + 1) * half], axis=0, keepdims=True) for l in range(levels)], axis=0
    )


def whole_kernel(
    alpha_hbm, kernel_hbm, src_hbm, dst_hbm, count_hbm, index_hbm, weight_hbm, pert_hbm, out_ref,
    prev_ref, alpha_ref, next_ref, kernel_ref, src_ref, dst_ref, count_ref, index_ref, weight_ref, pert_ref,
    rows, window, table, partial, slots,
    load_sem, halo_send, halo_recv, share_send, share_recv,
):
    tiles, owners = lax.axis_size("space"), lax.axis_size("members")
    tile, me = lax.axis_index("space"), lax.axis_index("members")
    right, left = lax.rem(tile + 1, tiles), lax.rem(tile + tiles - 1, tiles)
    span = out_ref.shape[1]
    blocks = alpha_ref.shape[2]

    barrier = pltpu.get_barrier_semaphore()
    for neighbour in (left, right):
        pl.semaphore_signal(barrier, inc=1, device_id={"space": neighbour}, device_id_type=MESH)
    for step in range(1, owners):
        peer = lax.rem(me + step, owners)
        pl.semaphore_signal(barrier, inc=1, device_id={"members": peer}, device_id_type=MESH)

    loads = []
    for number, (source, target) in enumerate((
        (alpha_hbm, alpha_ref), (kernel_hbm, kernel_ref), (src_hbm, src_ref), (dst_hbm, dst_ref),
        (count_hbm, count_ref), (index_hbm, index_ref), (weight_hbm, weight_ref), (pert_hbm, pert_ref),
    )):
        load = pltpu.make_async_copy(source, target, load_sem.at[number])
        load.start()
        loads.append(load)

    pl.semaphore_wait(barrier, owners + 1)
    halos = []
    for way, (neighbour, landing) in enumerate(((right, prev_ref), (left, next_ref))):
        copy = pltpu.make_async_remote_copy(
            src_ref=alpha_hbm,
            dst_ref=landing,
            send_sem=halo_send.at[way],
            recv_sem=halo_recv.at[way],
            device_id={"space": neighbour},
            device_id_type=MESH,
        )
        copy.start()
        halos.append(copy)
    loads[0].wait()
    stage(alpha_ref, 1, rows, window)
    for load in loads[1:]:
        load.wait()
    halos[0].wait_recv()
    stage(prev_ref, 0, rows, window)
    halos[1].wait_recv()
    stage(next_ref, 2, rows, window)
    convolve(src_ref, dst_ref, count_ref, blocks, kernel_ref, window, table)

    def share(step):
        return pltpu.make_async_remote_copy(
            src_ref=partial.at[step - 1],
            dst_ref=slots.at[step - 1],
            send_sem=share_send.at[step - 1],
            recv_sem=share_recv.at[step - 1],
            device_id={"members": lax.rem(me + step, owners)},
            device_id_type=MESH,
        )

    def columns(owner):
        return pl.ds(pl.multiple_of(owner * span, LANES), span)

    matrix = jnp.concatenate([table[0], table[1]], axis=1).astype(jnp.bfloat16)

    def body(step, carry):
        cols = columns(lax.rem(me + step, owners))
        partial[step - 1] = interpolate(matrix, cols, index_ref, weight_ref, pert_ref)

        @pl.when(step < owners)
        def _():
            share(step).start()

        return carry

    lax.fori_loop(1, owners + 1, body, 0)
    total = partial[owners - 1]
    for step in range(1, owners):
        share(step).wait_recv()
        total = total + slots[step - 1]
    out_ref[...] = total
    for step in range(1, owners):
        share(step).wait_send()
    for copy in halos:
        copy.wait_send()


def per_device(
    alpha, kernel, src_index, dst_index, entry_count, interp_index, interp_weight, perturbation
):
    owners = lax.axis_size("members")
    levels, members, blocks, width = alpha.shape
    lm = levels * members
    span = interp_index.shape[1] // owners
    operands = (
        alpha, kernel, src_index, dst_index, entry_count, interp_index, interp_weight,
        jnp.transpose(perturbation, (1, 0, 2)),
    )
    return pl.pallas_call(
        whole_kernel,
        out_shape=jax.ShapeDtypeStruct((levels, span), jnp.float32),
        in_specs=[pl.BlockSpec(memory_space=pl.ANY)] * len(operands),
        out_specs=pl.BlockSpec(memory_space=pltpu.VMEM),
        scratch_shapes=[
            pltpu.VMEM(alpha.shape, alpha.dtype),
            pltpu.VMEM(alpha.shape, alpha.dtype),
            pltpu.VMEM(alpha.shape, alpha.dtype),
            pltpu.VMEM(kernel.shape, kernel.dtype),
            pltpu.SMEM(src_index.shape, src_index.dtype),
            pltpu.SMEM(dst_index.shape, dst_index.dtype),
            pltpu.SMEM(entry_count.shape, entry_count.dtype),
            pltpu.VMEM(interp_index.shape, interp_index.dtype),
            pltpu.VMEM(interp_weight.shape, interp_weight.dtype),
            pltpu.VMEM(operands[-1].shape, perturbation.dtype),
            pltpu.VMEM((3, lm * blocks, width), jnp.float32),
            pltpu.VMEM((3 * blocks, lm, width), jnp.float32),
            pltpu.VMEM((2, lm * blocks // 2, width), jnp.float32),
            pltpu.VMEM((owners, levels, span), jnp.float32),
            pltpu.VMEM((owners - 1, levels, span), jnp.float32),
            pltpu.SemaphoreType.DMA((len(operands),)),
            pltpu.SemaphoreType.DMA((2,)),
            pltpu.SemaphoreType.DMA((2,)),
            pltpu.SemaphoreType.DMA((owners - 1,)),
            pltpu.SemaphoreType.DMA((owners - 1,)),
        ],
        compiler_params=pltpu.CompilerParams(
            collective_id=0, has_side_effects=True, vmem_limit_bytes=60 * 1024 * 1024
        ),
    )(*operands)


def solution(mesh):
    return jax.shard_map(
        per_device,
        mesh=mesh,
        in_specs=(
            P(None, "members", "space", None),
            P("space", None, None),
            P("space"),
            P("space"),
            P("space"),
            P(None, "space"),
            P(None, "space"),
            P(None, "members", "space"),
        ),
        out_specs=P(None, ("space", "members")),
        check_vma=False,
    )
```

```python
import jax
import jax.numpy as jnp
from jax import lax
from jax.experimental import pallas as pl
from jax.experimental.pallas import tpu as pltpu
from jax.sharding import PartitionSpec as P

MESH = pl.DeviceIdType.MESH
LANES = 128
PIECE = 256


def stage(ref, side, rows, window):
    levels, members, blocks, _ = ref.shape
    rows[side] = ref[...].astype(jnp.float32).reshape(levels * members * blocks, LANES)
    for j in range(blocks):
        window[side * blocks + j] = rows[side, pl.ds(j, levels * members, stride=blocks), :]


def convolve(src_ref, dst_ref, count_ref, blocks, kernel_ref, window, table):
    lm = window.shape[1]
    sums = [jnp.zeros((lm, LANES), jnp.float32) for _ in range(blocks)]
    for e in range(kernel_ref.shape[0]):
        piece = window[src_ref[e]].astype(jnp.bfloat16)
        product = jnp.dot(piece, kernel_ref[e], preferred_element_type=jnp.float32)
        live = jnp.where(e < count_ref[0], 1.0, 0.0).astype(jnp.float32)
        for j in range(blocks):
            factor = jnp.where(dst_ref[e] == j, live, 0.0)
            sums[j] = sums[j] + product * factor
    for j in range(blocks):
        table[pl.ds(j, lm, stride=blocks), :] = sums[j]


def interpolate(matrix, blocks, cols, index_ref, weight_ref, pert_ref):
    members, levels, _ = pert_ref.shape
    span = cols.size
    wide = (blocks, span)
    sub = lax.broadcasted_iota(jnp.int32, wide, 0)
    points = lax.broadcasted_iota(jnp.int16, (LANES, span), 0)
    total = None
    for k in range(index_ref.shape[0]):
        index = index_ref[pl.ds(k, 1), cols]
        weight = jnp.broadcast_to(weight_ref[pl.ds(k, 1), cols], wide)
        masked = jnp.where(jnp.broadcast_to(index >> 7, wide) == sub, weight, 0.0)
        place = jnp.broadcast_to(index & (LANES - 1), (16, span)).astype(jnp.int16)[0:1]
        hot = jnp.where(
            points == jnp.broadcast_to(place, (LANES, span)), jnp.bfloat16(1), jnp.bfloat16(0)
        )
        values = jnp.dot(matrix, hot, preferred_element_type=jnp.float32)
        values = values.reshape(levels * members, blocks, span) * masked[None]
        total = values if k == 0 else total + values
    sums = [None] * levels
    for m in range(members):
        p = pert_ref[m, :, cols].astype(jnp.float32)
        for l in range(levels):
            term = total[l * members + m] * jnp.broadcast_to(p[l:l + 1], wide)
            sums[l] = term if m == 0 else sums[l] + term
    return jnp.concatenate([jnp.sum(term, axis=0, keepdims=True) for term in sums], axis=0)


def whole_kernel(
    alpha_hbm, kernel_hbm, src_hbm, dst_hbm, count_hbm, index_hbm, weight_hbm, pert_hbm, out_ref,
    prev_ref, alpha_ref, next_ref, kernel_ref, src_ref, dst_ref, count_ref, index_ref, weight_ref, pert_ref,
    rows, window, table, partial, slots,
    load_sem, halo_send, halo_recv, share_send, share_recv,
):
    tiles, owners = lax.axis_size("space"), lax.axis_size("members")
    tile, me = lax.axis_index("space"), lax.axis_index("members")
    right, left = lax.rem(tile + 1, tiles), lax.rem(tile + tiles - 1, tiles)
    span = out_ref.shape[1]
    blocks = alpha_ref.shape[2]

    barrier = pltpu.get_barrier_semaphore()
    for neighbour in (left, right):
        pl.semaphore_signal(barrier, inc=1, device_id={"space": neighbour}, device_id_type=MESH)
    for step in range(1, owners):
        peer = lax.rem(me + step, owners)
        pl.semaphore_signal(barrier, inc=1, device_id={"members": peer}, device_id_type=MESH)

    loads = []
    for number, (source, target) in enumerate((
        (alpha_hbm, alpha_ref), (kernel_hbm, kernel_ref), (src_hbm, src_ref), (dst_hbm, dst_ref),
        (count_hbm, count_ref), (index_hbm, index_ref), (weight_hbm, weight_ref), (pert_hbm, pert_ref),
    )):
        load = pltpu.make_async_copy(source, target, load_sem.at[number])
        load.start()
        loads.append(load)

    pl.semaphore_wait(barrier, owners + 1)
    halos = []
    for way, (neighbour, landing) in enumerate(((right, prev_ref), (left, next_ref))):
        copy = pltpu.make_async_remote_copy(
            src_ref=alpha_hbm,
            dst_ref=landing,
            send_sem=halo_send.at[way],
            recv_sem=halo_recv.at[way],
            device_id={"space": neighbour},
            device_id_type=MESH,
        )
        copy.start()
        halos.append(copy)
    loads[0].wait()
    stage(alpha_ref, 1, rows, window)
    for load in loads[1:]:
        load.wait()
    halos[0].wait_recv()
    stage(prev_ref, 0, rows, window)
    halos[1].wait_recv()
    stage(next_ref, 2, rows, window)
    convolve(src_ref, dst_ref, count_ref, blocks, kernel_ref, window, table)

    def share(step):
        return pltpu.make_async_remote_copy(
            src_ref=partial.at[step - 1],
            dst_ref=slots.at[step - 1],
            send_sem=share_send.at[step - 1],
            recv_sem=share_recv.at[step - 1],
            device_id={"members": lax.rem(me + step, owners)},
            device_id_type=MESH,
        )

    matrix = table[...].astype(jnp.bfloat16)

    def body(step, carry):
        first = lax.rem(me + step, owners) * span
        for at in range(0, span, PIECE):
            cols = pl.ds(pl.multiple_of(first + at, LANES), PIECE)
            partial[step - 1, :, at:at + PIECE] = interpolate(
                matrix, blocks, cols, index_ref, weight_ref, pert_ref
            )

        @pl.when(step < owners)
        def _():
            share(step).start()

        return carry

    lax.fori_loop(1, owners + 1, body, 0)
    total = partial[owners - 1]
    for step in range(1, owners):
        share(step).wait_recv()
        total = total + slots[step - 1]
    out_ref[...] = total
    for step in range(1, owners):
        share(step).wait_send()
    for copy in halos:
        copy.wait_send()


def per_device(
    alpha, kernel, src_index, dst_index, entry_count, interp_index, interp_weight, perturbation
):
    owners = lax.axis_size("members")
    levels, members, blocks, width = alpha.shape
    lm = levels * members
    span = interp_index.shape[1] // owners
    operands = (
        alpha, kernel, src_index, dst_index, entry_count, interp_index, interp_weight,
        jnp.transpose(perturbation, (1, 0, 2)),
    )
    return pl.pallas_call(
        whole_kernel,
        out_shape=jax.ShapeDtypeStruct((levels, span), jnp.float32),
        in_specs=[pl.BlockSpec(memory_space=pl.ANY)] * len(operands),
        out_specs=pl.BlockSpec(memory_space=pltpu.VMEM),
        scratch_shapes=[
            pltpu.VMEM(alpha.shape, alpha.dtype),
            pltpu.VMEM(alpha.shape, alpha.dtype),
            pltpu.VMEM(alpha.shape, alpha.dtype),
            pltpu.VMEM(kernel.shape, kernel.dtype),
            pltpu.SMEM(src_index.shape, src_index.dtype),
            pltpu.SMEM(dst_index.shape, dst_index.dtype),
            pltpu.SMEM(entry_count.shape, entry_count.dtype),
            pltpu.VMEM(interp_index.shape, interp_index.dtype),
            pltpu.VMEM(interp_weight.shape, interp_weight.dtype),
            pltpu.VMEM(operands[-1].shape, perturbation.dtype),
            pltpu.VMEM((3, lm * blocks, width), jnp.float32),
            pltpu.VMEM((3 * blocks, lm, width), jnp.float32),
            pltpu.VMEM((lm * blocks, width), jnp.float32),
            pltpu.VMEM((owners, levels, span), jnp.float32),
            pltpu.VMEM((owners - 1, levels, span), jnp.float32),
            pltpu.SemaphoreType.DMA((len(operands),)),
            pltpu.SemaphoreType.DMA((2,)),
            pltpu.SemaphoreType.DMA((2,)),
            pltpu.SemaphoreType.DMA((owners - 1,)),
            pltpu.SemaphoreType.DMA((owners - 1,)),
        ],
        compiler_params=pltpu.CompilerParams(
            collective_id=0, has_side_effects=True, vmem_limit_bytes=60 * 1024 * 1024
        ),
    )(*operands)


def solution(mesh):
    return jax.shard_map(
        per_device,
        mesh=mesh,
        in_specs=(
            P(None, "members", "space", None),
            P("space", None, None),
            P("space"),
            P("space"),
            P("space"),
            P(None, "space"),
            P(None, "space"),
            P(None, "members", "space"),
        ),
        out_specs=P(None, ("space", "members")),
        check_vma=False,
    )
```

```python
import jax
import jax.numpy as jnp
from jax import lax
from jax.experimental import pallas as pl
from jax.experimental.pallas import tpu as pltpu
from jax.sharding import PartitionSpec as P

MESH = pl.DeviceIdType.MESH
LANES = 128
PIECE = 256


def stage(ref, side, rows, window):
    levels, members, blocks, _ = ref.shape
    rows[side] = ref[...].astype(jnp.float32).reshape(levels * members * blocks, LANES)
    for j in range(blocks):
        window[side * blocks + j] = rows[side, pl.ds(j, levels * members, stride=blocks), :]


def convolve(src_ref, dst_ref, count_ref, blocks, kernel_ref, window, table):
    lm = window.shape[1]
    sums = [jnp.zeros((lm, LANES), jnp.float32) for _ in range(blocks)]
    for e in range(kernel_ref.shape[0]):
        piece = window[src_ref[e]].astype(jnp.bfloat16)
        product = jnp.dot(piece, kernel_ref[e], preferred_element_type=jnp.float32)
        live = jnp.where(e < count_ref[0], 1.0, 0.0).astype(jnp.float32)
        for j in range(blocks):
            factor = jnp.where(dst_ref[e] == j, live, 0.0)
            sums[j] = sums[j] + product * factor
    for j in range(blocks):
        table[pl.ds(j, lm, stride=blocks), :] = sums[j]


def interpolate(matrix, blocks, cols, index_ref, weight_ref, pert_ref):
    members, levels, _ = pert_ref.shape
    span = cols.size
    wide = (blocks, span)
    sub = lax.broadcasted_iota(jnp.int32, wide, 0)
    points = lax.broadcasted_iota(jnp.int16, (LANES, span), 0)
    total = None
    for k in range(index_ref.shape[0]):
        index = index_ref[pl.ds(k, 1), cols]
        weight = jnp.broadcast_to(weight_ref[pl.ds(k, 1), cols], wide)
        masked = jnp.where(jnp.broadcast_to(index >> 7, wide) == sub, weight, 0.0)
        place = jnp.broadcast_to(index & (LANES - 1), (16, span)).astype(jnp.int16)[0:1]
        hot = jnp.where(
            points == jnp.broadcast_to(place, (LANES, span)), jnp.bfloat16(1), jnp.bfloat16(0)
        )
        values = jnp.dot(matrix, hot, preferred_element_type=jnp.float32)
        values = values.reshape(levels * members, blocks, span) * masked[None]
        total = values if k == 0 else total + values
    sums = [None] * levels
    for m in range(members):
        p = pert_ref[m, :, cols].astype(jnp.float32)
        for l in range(levels):
            term = total[l * members + m] * jnp.broadcast_to(p[l:l + 1], wide)
            sums[l] = term if m == 0 else sums[l] + term
    return jnp.concatenate([jnp.sum(term, axis=0, keepdims=True) for term in sums], axis=0)


def whole_kernel(
    alpha_hbm, kernel_hbm, src_hbm, dst_hbm, count_hbm, index_hbm, weight_hbm, pert_hbm, out_ref,
    prev_ref, alpha_ref, next_ref, kernel_ref, src_ref, dst_ref, count_ref, index_ref, weight_ref, pert_ref,
    rows, window, table, partial, slots,
    load_sem, ready, halo_send, halo_recv, share_send, share_recv,
):
    tiles, owners = lax.axis_size("space"), lax.axis_size("members")
    tile, me = lax.axis_index("space"), lax.axis_index("members")
    right, left = lax.rem(tile + 1, tiles), lax.rem(tile + tiles - 1, tiles)
    span = out_ref.shape[1]
    blocks = alpha_ref.shape[2]

    barrier = pltpu.get_barrier_semaphore()
    pl.semaphore_signal(barrier, inc=1, device_id={"space": left}, device_id_type=MESH)
    for step in range(1, owners):
        peer = lax.rem(me + step, owners)
        pl.semaphore_signal(barrier, inc=1, device_id={"members": peer}, device_id_type=MESH)

    loads = []
    for number, (source, target) in enumerate((
        (alpha_hbm, alpha_ref), (kernel_hbm, kernel_ref), (src_hbm, src_ref), (dst_hbm, dst_ref),
        (count_hbm, count_ref), (index_hbm, index_ref), (weight_hbm, weight_ref), (pert_hbm, pert_ref),
    )):
        load = pltpu.make_async_copy(source, target, load_sem.at[number])
        load.start()
        loads.append(load)

    pl.semaphore_wait(barrier, owners)
    pl.semaphore_signal(ready, inc=1, device_id={"space": right}, device_id_type=MESH)
    halos = []
    for way, (neighbour, landing) in enumerate(((right, prev_ref), (left, next_ref))):
        copy = pltpu.make_async_remote_copy(
            src_ref=alpha_hbm,
            dst_ref=landing,
            send_sem=halo_send.at[way],
            recv_sem=halo_recv.at[way],
            device_id={"space": neighbour},
            device_id_type=MESH,
        )
        if way == 1:
            pl.semaphore_wait(ready, 1)
        copy.start()
        halos.append(copy)
    loads[0].wait()
    stage(alpha_ref, 1, rows, window)
    for load in loads[1:]:
        load.wait()
    halos[0].wait_recv()
    stage(prev_ref, 0, rows, window)
    halos[1].wait_recv()
    stage(next_ref, 2, rows, window)
    convolve(src_ref, dst_ref, count_ref, blocks, kernel_ref, window, table)

    def share(step):
        return pltpu.make_async_remote_copy(
            src_ref=partial.at[step - 1],
            dst_ref=slots.at[step - 1],
            send_sem=share_send.at[step - 1],
            recv_sem=share_recv.at[step - 1],
            device_id={"members": lax.rem(me + step, owners)},
            device_id_type=MESH,
        )

    matrix = table[...].astype(jnp.bfloat16)

    def body(step, carry):
        first = lax.rem(me + step, owners) * span
        for at in range(0, span, PIECE):
            cols = pl.ds(pl.multiple_of(first + at, LANES), PIECE)
            partial[step - 1, :, at:at + PIECE] = interpolate(
                matrix, blocks, cols, index_ref, weight_ref, pert_ref
            )

        @pl.when(step < owners)
        def _():
            share(step).start()

        return carry

    lax.fori_loop(1, owners + 1, body, 0)
    total = partial[owners - 1]
    for step in range(1, owners):
        share(step).wait_recv()
        total = total + slots[step - 1]
    out_ref[...] = total
    for step in range(1, owners):
        share(step).wait_send()
    for copy in halos:
        copy.wait_send()


def per_device(
    alpha, kernel, src_index, dst_index, entry_count, interp_index, interp_weight, perturbation
):
    owners = lax.axis_size("members")
    levels, members, blocks, width = alpha.shape
    lm = levels * members
    span = interp_index.shape[1] // owners
    operands = (
        alpha, kernel, src_index, dst_index, entry_count, interp_index, interp_weight,
        jnp.transpose(perturbation, (1, 0, 2)),
    )
    return pl.pallas_call(
        whole_kernel,
        out_shape=jax.ShapeDtypeStruct((levels, span), jnp.float32),
        in_specs=[pl.BlockSpec(memory_space=pl.ANY)] * len(operands),
        out_specs=pl.BlockSpec(memory_space=pltpu.VMEM),
        scratch_shapes=[
            pltpu.VMEM(alpha.shape, alpha.dtype),
            pltpu.VMEM(alpha.shape, alpha.dtype),
            pltpu.VMEM(alpha.shape, alpha.dtype),
            pltpu.VMEM(kernel.shape, kernel.dtype),
            pltpu.SMEM(src_index.shape, src_index.dtype),
            pltpu.SMEM(dst_index.shape, dst_index.dtype),
            pltpu.SMEM(entry_count.shape, entry_count.dtype),
            pltpu.VMEM(interp_index.shape, interp_index.dtype),
            pltpu.VMEM(interp_weight.shape, interp_weight.dtype),
            pltpu.VMEM(operands[-1].shape, perturbation.dtype),
            pltpu.VMEM((3, lm * blocks, width), jnp.float32),
            pltpu.VMEM((3 * blocks, lm, width), jnp.float32),
            pltpu.VMEM((lm * blocks, width), jnp.float32),
            pltpu.VMEM((owners, levels, span), jnp.float32),
            pltpu.VMEM((owners - 1, levels, span), jnp.float32),
            pltpu.SemaphoreType.DMA((len(operands),)),
            pltpu.SemaphoreType.REGULAR,
            pltpu.SemaphoreType.DMA((2,)),
            pltpu.SemaphoreType.DMA((2,)),
            pltpu.SemaphoreType.DMA((owners - 1,)),
            pltpu.SemaphoreType.DMA((owners - 1,)),
        ],
        compiler_params=pltpu.CompilerParams(
            collective_id=0, has_side_effects=True, vmem_limit_bytes=60 * 1024 * 1024
        ),
    )(*operands)


def solution(mesh):
    return jax.shard_map(
        per_device,
        mesh=mesh,
        in_specs=(
            P(None, "members", "space", None),
            P("space", None, None),
            P("space"),
            P("space"),
            P("space"),
            P(None, "space"),
            P(None, "space"),
            P(None, "members", "space"),
        ),
        out_specs=P(None, ("space", "members")),
        check_vma=False,
    )
```

```python
import jax
import jax.numpy as jnp
from jax import lax
from jax.experimental import pallas as pl
from jax.experimental.pallas import tpu as pltpu
from jax.sharding import PartitionSpec as P

MESH = pl.DeviceIdType.MESH
LANES = 128
PIECE = 256


def stage(ref, side, rows, window):
    levels, members, blocks, _ = ref.shape
    rows[side] = ref[...].astype(jnp.float32).reshape(levels * members * blocks, LANES)
    for j in range(blocks):
        window[side * blocks + j] = rows[side, pl.ds(j, levels * members, stride=blocks), :]


def convolve(src_ref, dst_ref, count_ref, blocks, kernel_ref, window, table):
    lm = window.shape[1]
    sums = [jnp.zeros((lm, LANES), jnp.float32) for _ in range(blocks)]
    for e in range(kernel_ref.shape[0]):
        piece = window[src_ref[e]].astype(jnp.bfloat16)
        product = jnp.dot(piece, kernel_ref[e], preferred_element_type=jnp.float32)
        live = jnp.where(e < count_ref[0], 1.0, 0.0).astype(jnp.float32)
        for j in range(blocks):
            factor = jnp.where(dst_ref[e] == j, live, 0.0)
            sums[j] = sums[j] + product * factor
    for j in range(blocks):
        table[pl.ds(j, lm, stride=blocks), :] = sums[j]


def interpolate(matrix, blocks, cols, index_ref, weight_ref, pert_ref):
    members, levels, _ = pert_ref.shape
    span = cols.size
    wide = (blocks, span)
    sub = lax.broadcasted_iota(jnp.int32, wide, 0)
    points = lax.broadcasted_iota(jnp.int16, (LANES, span), 0)
    total = None
    for k in range(index_ref.shape[0]):
        index = index_ref[pl.ds(k, 1), cols]
        weight = jnp.broadcast_to(weight_ref[pl.ds(k, 1), cols], wide)
        masked = jnp.where(jnp.broadcast_to(index >> 7, wide) == sub, weight, 0.0)
        place = jnp.broadcast_to(index & (LANES - 1), (16, span)).astype(jnp.int16)[0:1]
        hot = jnp.where(
            points == jnp.broadcast_to(place, (LANES, span)), jnp.bfloat16(1), jnp.bfloat16(0)
        )
        values = jnp.dot(matrix, hot, preferred_element_type=jnp.float32)
        values = values.reshape(levels * members, blocks, span) * masked[None]
        total = values if k == 0 else total + values
    sums = [None] * levels
    for m in range(members):
        p = pert_ref[m, :, cols].astype(jnp.float32)
        for l in range(levels):
            term = total[l * members + m] * jnp.broadcast_to(p[l:l + 1], wide)
            sums[l] = term if m == 0 else sums[l] + term
    return jnp.concatenate([jnp.sum(term, axis=0, keepdims=True) for term in sums], axis=0)


def whole_kernel(
    alpha_hbm, kernel_hbm, src_hbm, dst_hbm, count_hbm, index_hbm, weight_hbm, pert_hbm, shares_ref,
    prev_ref, alpha_ref, next_ref, kernel_ref, src_ref, dst_ref, count_ref, index_ref, weight_ref, pert_ref,
    rows, window, table, partial,
    load_sem, own_sem, ready, halo_send, halo_recv, share_send, share_recv,
):
    tiles, owners = lax.axis_size("space"), lax.axis_size("members")
    tile, me = lax.axis_index("space"), lax.axis_index("members")
    right, left = lax.rem(tile + 1, tiles), lax.rem(tile + tiles - 1, tiles)
    span = shares_ref.shape[2]
    blocks = alpha_ref.shape[2]

    barrier = pltpu.get_barrier_semaphore()
    pl.semaphore_signal(barrier, inc=1, device_id={"space": left}, device_id_type=MESH)
    for step in range(1, owners):
        peer = lax.rem(me + step, owners)
        pl.semaphore_signal(barrier, inc=1, device_id={"members": peer}, device_id_type=MESH)

    loads = []
    for number, (source, target) in enumerate((
        (alpha_hbm, alpha_ref), (kernel_hbm, kernel_ref), (src_hbm, src_ref), (dst_hbm, dst_ref),
        (count_hbm, count_ref), (index_hbm, index_ref), (weight_hbm, weight_ref), (pert_hbm, pert_ref),
    )):
        load = pltpu.make_async_copy(source, target, load_sem.at[number])
        load.start()
        loads.append(load)

    pl.semaphore_wait(barrier, owners)
    pl.semaphore_signal(ready, inc=1, device_id={"space": right}, device_id_type=MESH)
    halos = []
    for way, (neighbour, landing) in enumerate(((right, prev_ref), (left, next_ref))):
        copy = pltpu.make_async_remote_copy(
            src_ref=alpha_hbm,
            dst_ref=landing,
            send_sem=halo_send.at[way],
            recv_sem=halo_recv.at[way],
            device_id={"space": neighbour},
            device_id_type=MESH,
        )
        if way == 1:
            pl.semaphore_wait(ready, 1)
        copy.start()
        halos.append(copy)
    loads[0].wait()
    stage(alpha_ref, 1, rows, window)
    for load in loads[1:]:
        load.wait()
    halos[1].wait_recv()
    stage(next_ref, 2, rows, window)
    halos[0].wait_recv()
    stage(prev_ref, 0, rows, window)
    convolve(src_ref, dst_ref, count_ref, blocks, kernel_ref, window, table)

    def share(step):
        return pltpu.make_async_remote_copy(
            src_ref=partial.at[step - 1],
            dst_ref=shares_ref.at[step - 1],
            send_sem=share_send.at[step - 1],
            recv_sem=share_recv.at[step - 1],
            device_id={"members": lax.rem(me + step, owners)},
            device_id_type=MESH,
        )

    matrix = table[...].astype(jnp.bfloat16)

    def body(step, carry):
        first = lax.rem(me + step, owners) * span
        for at in range(0, span, PIECE):
            cols = pl.ds(pl.multiple_of(first + at, LANES), PIECE)
            partial[step - 1, :, at:at + PIECE] = interpolate(
                matrix, blocks, cols, index_ref, weight_ref, pert_ref
            )

        @pl.when(step < owners)
        def _():
            share(step).start()

        return carry

    lax.fori_loop(1, owners + 1, body, 0)
    own = pltpu.make_async_copy(partial.at[owners - 1], shares_ref.at[owners - 1], own_sem)
    own.start()
    for step in range(1, owners):
        share(step).wait_recv()
    own.wait()
    for step in range(1, owners):
        share(step).wait_send()
    for copy in halos:
        copy.wait_send()


def per_device(
    alpha, kernel, src_index, dst_index, entry_count, interp_index, interp_weight, perturbation
):
    owners = lax.axis_size("members")
    levels, members, blocks, width = alpha.shape
    lm = levels * members
    span = interp_index.shape[1] // owners
    operands = (
        alpha, kernel, src_index, dst_index, entry_count, interp_index, interp_weight,
        jnp.transpose(perturbation, (1, 0, 2)),
    )
    shares = pl.pallas_call(
        whole_kernel,
        out_shape=jax.ShapeDtypeStruct((owners, levels, span), jnp.float32),
        in_specs=[pl.BlockSpec(memory_space=pl.ANY)] * len(operands),
        out_specs=pl.BlockSpec(memory_space=pl.ANY),
        scratch_shapes=[
            pltpu.VMEM(alpha.shape, alpha.dtype),
            pltpu.VMEM(alpha.shape, alpha.dtype),
            pltpu.VMEM(alpha.shape, alpha.dtype),
            pltpu.VMEM(kernel.shape, kernel.dtype),
            pltpu.SMEM(src_index.shape, src_index.dtype),
            pltpu.SMEM(dst_index.shape, dst_index.dtype),
            pltpu.SMEM(entry_count.shape, entry_count.dtype),
            pltpu.VMEM(interp_index.shape, interp_index.dtype),
            pltpu.VMEM(interp_weight.shape, interp_weight.dtype),
            pltpu.VMEM(operands[-1].shape, perturbation.dtype),
            pltpu.VMEM((3, lm * blocks, width), jnp.float32),
            pltpu.VMEM((3 * blocks, lm, width), jnp.float32),
            pltpu.VMEM((lm * blocks, width), jnp.float32),
            pltpu.VMEM((owners, levels, span), jnp.float32),
            pltpu.SemaphoreType.DMA((len(operands),)),
            pltpu.SemaphoreType.DMA,
            pltpu.SemaphoreType.REGULAR,
            pltpu.SemaphoreType.DMA((2,)),
            pltpu.SemaphoreType.DMA((2,)),
            pltpu.SemaphoreType.DMA((owners - 1,)),
            pltpu.SemaphoreType.DMA((owners - 1,)),
        ],
        compiler_params=pltpu.CompilerParams(
            collective_id=0, has_side_effects=True, vmem_limit_bytes=60 * 1024 * 1024
        ),
    )(*operands)
    return jnp.sum(shares, axis=0)


def solution(mesh):
    return jax.shard_map(
        per_device,
        mesh=mesh,
        in_specs=(
            P(None, "members", "space", None),
            P("space", None, None),
            P("space"),
            P("space"),
            P("space"),
            P(None, "space"),
            P(None, "space"),
            P(None, "members", "space"),
        ),
        out_specs=P(None, ("space", "members")),
        check_vma=False,
    )
```
